32 devices in a mesh: parts: 2 (over x), chan: 16 (over z, y, core).
Axes of the slice: x: 2, y: 2, z: 4, core: 2. Of those that a mesh axis runs over, the one named last changes fastest.
Arguments:
- spectra: bfloat16 [2, 256, 2, 2048], P(None, ('parts', 'chan')), parts along dimension 1, may hold values from -600 to 600
- pair_blocks: int32 [512, 2], P(('parts', 'chan')), parts along dimension 0, may hold values from 0 to 31, as said below
- pair_dest: int32 [512, 2], P(('parts', 'chan')), parts along dimension 0, may hold values from 0 to 15, as said below
- pair_count: int32 [32], P(('parts', 'chan')), parts along dimension 0, may hold values from 1 to 16, as said below
Outputs:
- stacks: float32 [512, 16, 4096], P(('parts', 'chan')), parts along dimension 0
The draws below stay inside these ranges and needn't reach their ends.
There are 2 independent parts, one for each index of `parts`. The reference program is written for one: setup_inputs(seed, part) draws one part's arguments, and reference() takes and returns one part's arrays. A program takes and returns all parts, laid end to end along the dimension named above; each array names one. Nothing has to cross between parts.
Inputs may be any that keep to these rules, and one draw needn't show every extreme that they name: `pair_blocks`: every row r names a first block a with (r div 16) * 2 <= a < (r div 16 + 1) * 2, and a second block b with |a - b| <= 2; that distance occurs in a used row. `pair_dest`: the used rows of one device name distinct owners; no two used rows name the same owner and slot; some owner receives a used row from every device. `pair_count`: some device uses all 16 of its rows.
All inputs are finite; a program needn't handle non-finite values.
Results may differ from the reference program's by a relative error of at most 0.0057.
Values may be sent and summed in bfloat16 or wider, within the bound.
A program may use at most 640 MiB of HBM per device.

```python
import math
import jax
import jax.numpy as jnp
from jax import lax

LAGS = 4096
FREQ = 2048
CH = 4
BLK_DEV = 2
SEG = 2
BLOCKS = 32
CHANNELS = 128
REACH = 2
SLOTS = 16


def draw_spectra(key, part):
    base_key = jax.random.fold_in(key, 101)
    subkeys = jax.random.split(base_key, 3)
    shape_all = (SEG, CHANNELS, 2, FREQ)
    noise = jnp.clip(jax.random.normal(subkeys[0], shape_all, jnp.float32), -6.0, 6.0)
    top_log = math.log(10.0)
    row_scales = jnp.exp(jax.random.uniform(subkeys[1], (SEG, CHANNELS, 1, 1), jnp.float32, 0.0, top_log))
    col_scales = jnp.exp(jax.random.uniform(subkeys[2], (1, 1, 1, FREQ), jnp.float32, 0.0, math.log(10.0)))
    return (noise * row_scales * col_scales).astype(jnp.bfloat16)


def lists_common(key):
    base_key = jax.random.fold_in(key, 907)
    subkeys = jax.random.split(base_key, 8)
    dev_count = SLOTS
    full_owner = jax.random.randint(subkeys[0], (), 0, dev_count)
    busy_dev = jax.random.randint(subkeys[1], (), 0, dev_count)
    places = jnp.arange(dev_count, dtype=jnp.int32)
    counts = jax.random.randint(subkeys[2], (dev_count,), max(1, dev_count // 8), dev_count // 2 + 1)
    counts = jnp.where(places == busy_dev, dev_count, counts).astype(jnp.int32)
    scores = jax.random.randint(subkeys[3], (dev_count, dev_count), 0, 1 << 20)
    scores = jnp.where(places[None, :] == full_owner, -1, scores)
    owner_order = jnp.argsort(scores, axis=1, stable=True).astype(jnp.int32)
    offset = jax.random.randint(subkeys[4], (dev_count,), 0, 1 << 20) % counts
    moved_pos = jnp.where(places[None, :] < counts[:, None], (places[None, :] + offset[:, None]) % counts[:, None], places[None, :])
    owners = jnp.take_along_axis(owner_order, moved_pos.astype(jnp.int32), axis=1)
    ranking = jnp.argsort(jax.random.randint(subkeys[5], (dev_count, dev_count), 0, 1 << 20), axis=1, stable=True).astype(jnp.int32)
    slot_ids = ranking[owners, places[:, None]]
    destinations = jnp.stack([owners, slot_ids], axis=-1).reshape(dev_count * dev_count, 2).astype(jnp.int32)
    row_count = dev_count * dev_count
    row_index = jnp.arange(row_count, dtype=jnp.int32)
    row_dev = row_index // dev_count
    first_block = row_dev * BLK_DEV + jax.random.randint(subkeys[6], (row_count,), 0, BLK_DEV)
    low_bound = jnp.maximum(first_block - REACH, 0)
    high_bound = jnp.minimum(first_block + REACH, BLOCKS - 1)
    second = jax.random.randint(subkeys[7], (row_count,), low_bound, high_bound + 1)
    upward = busy_dev * BLK_DEV + REACH <= BLOCKS - 1
    far_first = jnp.where(upward, busy_dev * BLK_DEV, busy_dev * BLK_DEV + BLK_DEV - 1)
    far_second = jnp.where(upward, far_first + REACH, far_first - REACH)
    row_far = busy_dev * dev_count
    first_block = jnp.where(row_index == row_far, far_first, first_block)
    second = jnp.where(row_index == row_far, far_second, second)
    blocks = jnp.stack([first_block, second], axis=-1).astype(jnp.int32)
    return (blocks, destinations, counts)


def draw_pair_blocks(key, part):
    return lists_common(key)[0]


def draw_pair_dest(key, part):
    return lists_common(key)[1]


def draw_pair_count(key, part):
    return lists_common(key)[2]


def setup_inputs(seed: int = 0, part: int = 0) -> dict:
    seeds = jax.random.split(jax.random.key(seed), 5)
    part_keys = jax.random.split(jax.random.fold_in(seeds[4], part), 5)
    spectra = draw_spectra(jax.random.fold_in(jax.random.fold_in(seeds[4], part), 71), part)
    pair_blocks = draw_pair_blocks(jax.random.fold_in(jax.random.fold_in(seeds[4], part), 71), part)
    pair_dest = draw_pair_dest(jax.random.fold_in(jax.random.fold_in(seeds[4], part), 71), part)
    pair_count = draw_pair_count(jax.random.fold_in(jax.random.fold_in(seeds[4], part), 71), part)
    return dict(spectra=spectra, pair_blocks=pair_blocks, pair_dest=pair_dest, pair_count=pair_count)


def make_basis(bin_count, lags):
    freq_bins = jnp.arange(bin_count, dtype=jnp.int32)
    delays = jnp.arange(lags, dtype=jnp.int32)
    quarter = jnp.arange(2, dtype=jnp.int32) * (lags // 4)
    phase_index = (freq_bins[None, :, None] * delays[None, None, :] + quarter[:, None, None]) % lags
    angles = phase_index.astype(jnp.float32) * (2.0 * math.pi / lags)
    weight = jnp.where(freq_bins == 0, 1.0, 2.0).astype(jnp.float32)[None, :, None] / (2.0 * math.sqrt(bin_count))
    return (weight * jnp.cos(angles)).astype(jnp.bfloat16).reshape(2 * bin_count, lags)

def whiten(spectra):
    values = spectra.astype(jnp.float32)
    mean_power = lax.optimization_barrier(jnp.mean(values * values, axis=(2, 3), keepdims=True))
    return (values / jnp.sqrt(mean_power + 1e-06)).astype(jnp.bfloat16)

def cross_rows(whitened, blocks, weights):
    segments, channels, two_sides, bin_count = whitened.shape
    grouped = whitened.reshape(segments, channels // CH, CH, two_sides, bin_count)
    first_side = jnp.take(grouped, blocks[:, 0], axis=1).astype(jnp.float32)
    second_side = jnp.take(grouped, blocks[:, 1], axis=1).astype(jnp.float32)
    left_real = first_side[:, :, :, 0, :][:, :, :, None, :]
    left_imag = first_side[:, :, :, 1, :][:, :, :, None, :]
    right_real = second_side[:, :, :, 0, :][:, :, None, :, :]
    right_imag = second_side[:, :, :, 1, :][:, :, None, :, :]
    real_part = lax.optimization_barrier(jnp.sum(left_real * right_real + left_imag * right_imag, axis=0))
    imag_part = lax.optimization_barrier(jnp.sum(left_imag * right_real - left_real * right_imag, axis=0))
    row_scale = weights.astype(jnp.float32) / segments
    stacked = jnp.stack([real_part, imag_part], axis=3) * row_scale[:, None, None, None, None]
    return stacked.astype(jnp.bfloat16).reshape(blocks.shape[0] * CH * CH, two_sides * bin_count)

def reference(spectra, pair_blocks, pair_dest, pair_count):
    whitened = whiten(spectra)
    lag_basis = make_basis(FREQ, LAGS)
    row_index = jnp.arange(SLOTS * SLOTS, dtype=jnp.int32)
    valid = row_index % SLOTS < pair_count[row_index // SLOTS]
    blocks_dev = pair_blocks.reshape(SLOTS, SLOTS, 2)
    valid_dev = valid.reshape(SLOTS, SLOTS)

    def one_device(device_item):
        blocks, weights = device_item
        matrix = cross_rows(whitened, blocks, weights)
        return jnp.dot(matrix, lag_basis, preferred_element_type=jnp.float32).reshape(SLOTS, CH * CH, LAGS)
    correlation = lax.map(one_device, (blocks_dev, valid_dev))
    target = pair_dest[:, 0] * SLOTS + pair_dest[:, 1]
    target = jnp.where(valid, target, SLOTS * SLOTS).astype(jnp.int32)
    stacks = jnp.zeros((SLOTS * SLOTS, CH * CH, LAGS), jnp.float32)
    stacks = stacks.at[target].add(correlation.reshape(SLOTS * SLOTS, CH * CH, LAGS), mode='drop')
    return stacks
```

```python
import functools
import math

import jax
import jax.numpy as jnp
import ml_dtypes
import numpy as np
from jax import lax
from jax.experimental import pallas as pl
from jax.experimental.pallas import tpu as pltpu
from jax.sharding import PartitionSpec as P

LAGS = 4096
FREQ = 2048
CH = 4
RADIX = 16
BINS = FREQ // RADIX
SPAN = LAGS // RADIX
PAIRS = RADIX // 2
MESH = pl.DeviceIdType.MESH


def stage_basis():
    fb = np.arange(BINS)
    nb = np.arange(SPAN)

    def parts(fa):
        f = fa + RADIX * fb
        weight = np.where(f == 0, 1.0, 2.0)[:, None] / (2.0 * math.sqrt(FREQ))
        angle = (f[:, None] * nb[None, :] % LAGS) * (2.0 * math.pi / LAGS)
        c, s = weight * np.cos(angle), weight * np.sin(angle)
        return np.concatenate([c, -s]), np.concatenate([s, c])

    out = np.zeros((PAIRS, 4 * BINS, 2 * SPAN))
    for q in range(PAIRS):
        low = parts(q)
        high = parts(RADIX - q if q else PAIRS)
        if q:
            out[q] = np.block([[low[0], low[1]], [high[0], -high[1]]])
        else:
            zero = np.zeros_like(low[0])
            out[q] = np.block([[low[0], zero], [zero, high[0]]])
    return out.astype(ml_dtypes.bfloat16)


def gather_kernel(n, x_ref, meta_ref, all_ref, piece, own_sem, send_sems, recv_sems):
    me = lax.axis_index("chan")
    nz = n // 4
    z, y, c = me // 4, (me // 2) % 2, me % 2

    def index(zz, yy, cc):
        return (zz * 2 + yy) * 2 + cc

    def far(k):
        out, bit = 0, 1
        while bit < nz:
            out = out + (((z // bit) + (k // bit)) % 2) * bit
            bit *= 2
        return out

    zs = [far(k) for k in range(1, nz)]
    other_y, other_c = index(z, 1 - y, c), index(z, y, 1 - c)
    partners = [index(zz, y, c) for zz in zs] + [other_y, other_c]
    barrier = pltpu.get_barrier_semaphore()
    for dev in partners:
        pl.semaphore_signal(barrier, inc=1, device_id={"chan": dev}, device_id_type=MESH)

    rows = x_ref.shape[0]
    half = rows // 2
    values = x_ref[...].astype(jnp.float32)
    power = jnp.sum(values * values, axis=1, keepdims=True)
    mean_power = (power[:half] + power[half:]) * (1.0 / (2 * FREQ))
    root = jnp.sqrt(mean_power + 1e-06)
    white = (values / jnp.concatenate([root, root], axis=0)).astype(jnp.bfloat16)
    groups = FREQ // 256
    stacked = jnp.concatenate([white[:, g * 256 : (g + 1) * 256] for g in range(groups)], axis=0)
    src = lax.broadcasted_iota(jnp.int32, (256, 256), 0)
    dst = lax.broadcasted_iota(jnp.int32, (256, 256), 1)
    perm = ((src & 15) * 16 + (src >> 4) == dst).astype(jnp.float32).astype(jnp.bfloat16)
    sorted_bins = jnp.dot(stacked, perm, preferred_element_type=jnp.float32)
    place = lax.broadcasted_iota(jnp.int32, (rows, 128), 1) >> 4
    for h in range(2):
        turned = []
        for g in range(groups):
            t = sorted_bins[g * rows : (g + 1) * rows, h * 128 : (h + 1) * 128]
            turned.append(pltpu.roll(t, g * 16, 1) if g else t)
        for fl in range(8):
            t = turned[0]
            for g in range(1, groups):
                t = jnp.where(place == (fl + g) % 8, turned[g], t)
            if fl:
                t = pltpu.roll(t, 128 - fl * 16, 1)
            t = t.astype(jnp.bfloat16)
            piece[h * 8 + fl, :, 0:128] = t[:half]
            piece[h * 8 + fl, :, 128:256] = t[half:]
    piece[RADIX] = meta_ref[...]

    own = pltpu.make_async_copy(piece, all_ref.at[me], own_sem)
    own.start()
    pl.semaphore_wait(barrier, len(partners))
    copies = []

    def send(what, dev, src_ref=None):
        copy = pltpu.make_async_remote_copy(
            src_ref=all_ref.at[what] if src_ref is None else src_ref,
            dst_ref=all_ref.at[what],
            send_sem=send_sems.at[len(copies)],
            recv_sem=recv_sems.at[what],
            device_id={"chan": dev},
            device_id_type=MESH,
        )
        copy.start()
        copies.append(copy)

    def arrived(what):
        pltpu.make_async_remote_copy(
            src_ref=all_ref.at[what],
            dst_ref=all_ref.at[what],
            send_sem=send_sems.at[0],
            recv_sem=recv_sems.at[what],
            device_id={"chan": other_c},
            device_id_type=MESH,
        ).wait_recv()

    send(me, other_y, piece)
    for zz in zs:
        send(me, index(zz, y, c), piece)
    send(me, other_c, piece)
    arrived(other_y)
    send(other_y, other_c)
    for zz in zs:
        what = index(zz, y, c)
        arrived(what)
        send(what, other_y)
        send(what, other_c)
    for zz in zs:
        what = index(zz, 1 - y, c)
        arrived(what)
        send(what, other_c)
    for zz in [z] + zs:
        for yy in (y, 1 - y):
            arrived(index(zz, yy, 1 - c))
    own.wait()
    for copy in copies:
        copy.wait_send()


def gather(n, x, meta):
    rows = x.shape[0] // 2
    shape = (RADIX + 1, rows, 2 * BINS)
    return pl.pallas_call(
        functools.partial(gather_kernel, n),
        out_shape=jax.ShapeDtypeStruct((n,) + shape, jnp.bfloat16),
        in_specs=[pl.BlockSpec(memory_space=pltpu.VMEM)] * 2,
        out_specs=pl.BlockSpec(memory_space=pl.ANY),
        scratch_shapes=[
            pltpu.VMEM(shape, jnp.bfloat16),
            pltpu.SemaphoreType.DMA,
            pltpu.SemaphoreType.DMA((n - 1,)),
            pltpu.SemaphoreType.DMA((n,)),
        ],
        compiler_params=pltpu.CompilerParams(
            collective_id=0, has_side_effects=True, vmem_limit_bytes=16 * 1024 * 1024
        ),
    )(x, meta)


def transform(coef, put):
    cos = [math.cos(2 * math.pi * k / 16) for k in range(16)]
    sin = [math.sin(2 * math.pi * k / 16) for k in range(16)]
    a = [coef(0)] + [coef(2 * q) for q in range(1, 8)]
    b = [None] + [coef(2 * q + 1) for q in range(1, 8)]
    a8 = coef(1)
    s08, d08 = a[0] + a8, a[0] - a8
    ee = [s08 + a[4], d08 - b[4], s08 - a[4], d08 + b[4]]
    sa, da, sb, db = a[2] + a[6], a[2] - a[6], b[2] + b[6], b[2] - b[6]
    r = cos[2]
    eo = [sa, r * (da - sb), -db, -(r * (da + sb))]
    even = [ee[k] + eo[k] for k in range(4)] + [ee[k] - eo[k] for k in range(4)]
    p1, m1, p3, m3 = a[1] + a[7], a[1] - a[7], a[3] + a[5], a[3] - a[5]
    bp1, bm1, bp3, bm3 = b[1] + b[7], b[1] - b[7], b[3] + b[5], b[3] - b[5]
    for k in range(8):
        u1, u3 = (p1, p3) if k % 2 == 0 else (m1, m3)
        v1, v3 = (bm1, bm3) if k % 2 == 0 else (bp1, bp3)
        k3 = 3 * k % 16
        if k == 0:
            odd = u1 + u3
        elif k == 4:
            odd = v3 - v1
        else:
            odd = cos[k] * u1 - sin[k] * v1 + cos[k3] * u3 - sin[k3] * v3
        put(k, even[k] + odd)
        put(k + 8, even[k] - odd)


def stack_kernel(n, slots, chunk, low_ref, high_ref, meta_ref, basis_ref, out_ref, pick, coefs):
    step = pl.program_id(0)
    rows = slots * CH * CH
    depth = n * low_ref.shape[2]

    @pl.when(step == 0)
    def _():
        me = lax.axis_index("chan").astype(jnp.float32)
        slot = lax.broadcasted_iota(jnp.int32, (slots, 2 * BINS), 0).astype(jnp.float32)
        found_a = jnp.zeros((slots, 2 * BINS), jnp.float32)
        found_b = jnp.zeros((slots, 2 * BINS), jnp.float32)
        for d in range(n):
            lists = meta_ref[d, 0].astype(jnp.float32)
            here = jnp.logical_and(lists[0:1] == me, lists[1:2] == slot)
            found_a = jnp.where(here, lists[2:3], found_a)
            found_b = jnp.where(here, lists[3:4], found_b)

        def spread(found):
            total = jnp.sum(found, axis=1, keepdims=True) - 1.0
            wide = jnp.broadcast_to(total, (slots, depth))
            wide = jnp.broadcast_to(wide[:, None, :], (slots, CH * CH, depth))
            return wide.reshape(rows, depth).astype(jnp.int32)

        row = lax.broadcasted_iota(jnp.int32, (rows, depth), 0)
        column = lax.broadcasted_iota(jnp.int32, (rows, depth), 1)
        channel = (column >> 4) * 8 + (column & 7)
        segment = (column >> 3) & 1
        for side, found in enumerate((found_a, found_b)):
            member = (row >> 2) & 3 if side == 0 else row & 3
            same = channel == spread(found) * CH + member
            for s in range(2):
                hit = jnp.where(jnp.logical_and(same, segment == s), 1.0, 0.0)
                k = (side * 2 + s) * rows
                pick[k : k + rows, :] = hit.astype(jnp.bfloat16)

    @pl.when(step < PAIRS)
    def _():
        crosses = []
        for ref in (low_ref, high_ref):
            white = ref[:, 0].reshape(depth, 2 * BINS)
            found = jnp.dot(pick[...], white, preferred_element_type=jnp.float32)
            re, im = 0.0, 0.0
            for s in range(2):
                left = found[s * rows : (s + 1) * rows]
                right = found[(2 + s) * rows : (3 + s) * rows]
                l0, l1 = left[:, :BINS], left[:, BINS:]
                r0, r1 = right[:, :BINS], right[:, BINS:]
                re = re + (l0 * r0 + l1 * r1)
                im = im + (l1 * r0 - l0 * r1)
            crosses += [(re * 0.5).astype(jnp.bfloat16), (im * 0.5).astype(jnp.bfloat16)]
        cross = jnp.concatenate(crosses, axis=1)
        coefs[step] = jnp.dot(cross, basis_ref[0], preferred_element_type=jnp.float32)

    @pl.when(step >= PAIRS)
    def _():
        base = (step - PAIRS) * chunk

        def body(i, carry):
            for h in range(SPAN // 128):
                def coef(k):
                    col = (k % 2) * SPAN + h * 128
                    at = pl.ds(pl.multiple_of(base + i * 8, 8), 8)
                    return coefs[k // 2, at, col : col + 128]

                def put(na, value):
                    col = na * SPAN + h * 128
                    out_ref[pl.ds(pl.multiple_of(i * 8, 8), 8), col : col + 128] = value

                transform(coef, put)
            return carry

        lax.fori_loop(0, chunk // 8, body, 0)


def stack(n, slots, pieces, basis):
    rows = slots * CH * CH
    half = pieces.shape[2]
    chunk = 64
    block = (n, 1, half, 2 * BINS)

    def low(i):
        return (0, jnp.minimum(i, PAIRS - 1), 0, 0)

    def high(i):
        return (0, jnp.where(i == 0, PAIRS, jnp.maximum(RADIX - i, PAIRS + 1)), 0, 0)

    return pl.pallas_call(
        functools.partial(stack_kernel, n, slots, chunk),
        out_shape=jax.ShapeDtypeStruct((rows, LAGS), jnp.float32),
        grid=(PAIRS + rows // chunk,),
        in_specs=[
            pl.BlockSpec(block, low),
            pl.BlockSpec(block, high),
            pl.BlockSpec(block, lambda i: (0, RADIX, 0, 0)),
            pl.BlockSpec((1, 4 * BINS, 2 * SPAN), lambda i: (jnp.minimum(i, PAIRS - 1), 0, 0)),
        ],
        out_specs=pl.BlockSpec((chunk, LAGS), lambda i: (jnp.maximum(i - PAIRS, 0), 0)),
        scratch_shapes=[
            pltpu.VMEM((4 * rows, n * half), jnp.bfloat16),
            pltpu.VMEM((PAIRS, rows, 2 * SPAN), jnp.float32),
        ],
        compiler_params=pltpu.CompilerParams(vmem_limit_bytes=40 * 1024 * 1024),
    )(pieces, pieces, pieces, basis)


def shards(basis, spectra, pair_blocks, pair_dest, pair_count):
    slots = pair_dest.shape[0]
    n = lax.axis_size("chan")
    x = spectra.transpose(2, 0, 1, 3).reshape(-1, FREQ)
    used = jnp.arange(slots, dtype=jnp.int32) < pair_count[0]
    lists = jnp.stack(
        [
            jnp.where(used, pair_dest[:, 0], -1),
            pair_dest[:, 1],
            pair_blocks[:, 0] + 1,
            pair_blocks[:, 1] + 1,
        ]
    )
    half = x.shape[0] // 2
    meta = jnp.pad(
        lists, ((0, half - 4), (0, 2 * BINS - slots)), constant_values=-1
    ).astype(jnp.bfloat16)
    pieces = gather(n, x, meta)
    out = stack(n, slots, pieces, jnp.asarray(basis))
    return out.reshape(slots, CH * CH, LAGS)


def solution(mesh):
    in_specs = (
        P(None, ("parts", "chan"), None, None),
        P(("parts", "chan"), None),
        P(("parts", "chan"), None),
        P(("parts", "chan")),
    )
    out_specs = P(("parts", "chan"), None, None)
    return jax.shard_map(
        functools.partial(shards, stage_basis()),
        mesh=mesh,
        in_specs=in_specs,
        out_specs=out_specs,
        check_vma=False,
    )
```

```python
import functools
import math

import jax
import jax.numpy as jnp
import ml_dtypes
import numpy as np
from jax import lax
from jax.experimental import pallas as pl
from jax.experimental.pallas import tpu as pltpu
from jax.sharding import PartitionSpec as P

LAGS = 4096
FREQ = 2048
CH = 4
RADIX = 16
BINS = FREQ // RADIX
SPAN = LAGS // RADIX
PAIRS = RADIX // 2
MESH = pl.DeviceIdType.MESH


def stage_basis():
    fb = np.arange(BINS)
    nb = np.arange(SPAN)

    def parts(fa):
        f = fa + RADIX * fb
        weight = np.where(f == 0, 1.0, 2.0)[:, None] / (2.0 * math.sqrt(FREQ))
        angle = (f[:, None] * nb[None, :] % LAGS) * (2.0 * math.pi / LAGS)
        c, s = weight * np.cos(angle), weight * np.sin(angle)
        return np.concatenate([c, -s]), np.concatenate([s, c])

    out = np.zeros((PAIRS, 4 * BINS, 2 * SPAN))
    for q in range(PAIRS):
        low = parts(q)
        high = parts(RADIX - q if q else PAIRS)
        if q:
            out[q] = np.block([[low[0], low[1]], [high[0], -high[1]]])
        else:
            zero = np.zeros_like(low[0])
            out[q] = np.block([[low[0], zero], [zero, high[0]]])
    return out.astype(ml_dtypes.bfloat16)


def tile_of(fa):
    if fa % PAIRS == 0:
        return fa // PAIRS
    return 2 * fa if fa < PAIRS else 2 * (RADIX - fa) + 1


def gather_kernel(
    n, count_ref, x_ref, dest_ref, blocks_ref, all_ref, lists, piece, own_sem, send_sems, recv_sems
):
    me = lax.axis_index("chan")
    nz = n // 4
    z, y, c = me // 4, (me // 2) % 2, me % 2
    always, up, down = None, z < nz - 1, z > 0

    def index(zz, yy, cc):
        return (zz * 2 + yy) * 2 + cc

    def under(condition, body):
        if condition is None:
            body()
        else:
            pl.when(condition)(body)

    other_y, other_c = index(z, 1 - y, c), index(z, y, 1 - c)
    above, below = index(z + 1, y, c), index(z - 1, y, c)
    partners = [(always, other_y), (always, other_c), (up, above), (down, below)]
    barrier = pltpu.get_barrier_semaphore()
    for condition, dev in partners:
        under(
            condition,
            lambda dev=dev: pl.semaphore_signal(
                barrier, inc=1, device_id={"chan": dev}, device_id_type=MESH
            ),
        )

    slots = dest_ref.shape[1]
    used = lax.broadcasted_iota(jnp.int32, (1, slots), 1) < count_ref[0]
    lists[...] = jnp.full(lists.shape, -1.0, jnp.float32)
    lists[0:1, 0:slots] = jnp.where(used, dest_ref[0:1, :], -1).astype(jnp.float32)
    lists[1:2, 0:slots] = dest_ref[1:2, :].astype(jnp.float32)
    lists[2:4, 0:slots] = (blocks_ref[...] + 1).astype(jnp.float32)
    piece[RADIX] = lists[...].astype(jnp.bfloat16)
    rows = x_ref.shape[0]
    half = rows // 2
    values = x_ref[...].astype(jnp.float32)
    power = jnp.sum(values * values, axis=1, keepdims=True)
    mean_power = (power[:half] + power[half:]) * (1.0 / (2 * FREQ))
    root = jnp.sqrt(mean_power + 1e-06)
    white = (values / jnp.concatenate([root, root], axis=0)).astype(jnp.bfloat16)
    groups = FREQ // 256
    stacked = jnp.concatenate([white[:, g * 256 : (g + 1) * 256] for g in range(groups)], axis=0)
    src = lax.broadcasted_iota(jnp.int32, (256, 256), 0)
    dst = lax.broadcasted_iota(jnp.int32, (256, 256), 1)
    perm = ((src & 15) * 16 + (src >> 4) == dst).astype(jnp.float32).astype(jnp.bfloat16)
    sorted_bins = jnp.dot(stacked, perm, preferred_element_type=jnp.float32)
    place = lax.broadcasted_iota(jnp.int32, (rows, 128), 1) >> 4
    for h in range(2):
        turned = []
        for g in range(groups):
            t = sorted_bins[g * rows : (g + 1) * rows, h * 128 : (h + 1) * 128]
            turned.append(pltpu.roll(t, g * 16, 1) if g else t)
        for fl in range(8):
            t = turned[0]
            for g in range(1, groups):
                t = jnp.where(place == (fl + g) % 8, turned[g], t)
            if fl:
                t = pltpu.roll(t, 128 - fl * 16, 1)
            t = t.astype(jnp.bfloat16)
            piece[tile_of(h * 8 + fl), :, 0:128] = t[:half]
            piece[tile_of(h * 8 + fl), :, 128:256] = t[half:]

    own = pltpu.make_async_copy(piece, all_ref.at[me], own_sem)
    own.start()
    pl.semaphore_wait(barrier, 2 + (z + nz - 1) // nz + (2 * nz - 2 - z) // nz)
    halves = [pl.ds(PAIRS, PAIRS + 1), pl.ds(0, PAIRS)]
    copies = []

    def both(first, second):
        if first is None or second is None:
            return second if first is None else first
        return jnp.logical_and(first, second)

    def send(condition, k, what, dev, src_ref=None):
        copy = pltpu.make_async_remote_copy(
            src_ref=(all_ref.at[what] if src_ref is None else src_ref).at[halves[k]],
            dst_ref=all_ref.at[what, halves[k]],
            send_sem=send_sems.at[len(copies)],
            recv_sem=recv_sems.at[k, what],
            device_id={"chan": dev},
            device_id_type=MESH,
        )
        copies.append((condition, copy))
        under(condition, copy.start)

    def arrived(condition, k, what):
        under(
            condition,
            pltpu.make_async_remote_copy(
                src_ref=all_ref.at[what, halves[k]],
                dst_ref=all_ref.at[what, halves[k]],
                send_sem=send_sems.at[0],
                recv_sem=recv_sems.at[k, what],
                device_id={"chan": other_c},
                device_id_type=MESH,
            ).wait_recv,
        )

    for k in range(2):
        send(always, k, me, other_y, piece)
        send(up, k, me, above, piece)
        send(down, k, me, below, piece)
        send(always, k, me, other_c, piece)
    for t in range(1, nz + 1):
        for k in range(2):
            for onward, there, zz, dev in (
                (up, z >= t, z - t, above),
                (down, z < nz - t, z + t, below),
            ):
                if t < nz:
                    what = index(zz, y, c)
                    arrived(there, k, what)
                    send(there, k, what, other_y)
                    if t < nz - 1:
                        send(both(there, onward), k, what, dev)
                    send(there, k, what, other_c)
        for k in range(2):
            if t == 1:
                arrived(always, k, other_y)
                send(always, k, other_y, other_c)
            else:
                for there, zz in ((z >= t - 1, z - t + 1), (z < nz - t + 1, z + t - 1)):
                    what = index(zz, 1 - y, c)
                    arrived(there, k, what)
                    send(there, k, what, other_c)
    for k in range(2):
        for zz in range(nz):
            for yy in range(2):
                arrived(always, k, index(zz, yy, 1 - c))
    own.wait()
    for condition, copy in copies:
        under(condition, copy.wait_send)


def gather(n, count, x, dest, blocks):
    half = x.shape[0] // 2
    shape = (RADIX + 1, half, 2 * BINS)
    vmem = pl.BlockSpec(memory_space=pltpu.VMEM)
    return pl.pallas_call(
        functools.partial(gather_kernel, n),
        out_shape=jax.ShapeDtypeStruct((n,) + shape, jnp.bfloat16),
        in_specs=[pl.BlockSpec(memory_space=pltpu.SMEM), vmem, vmem, vmem],
        out_specs=pl.BlockSpec(memory_space=pl.ANY),
        scratch_shapes=[
            pltpu.VMEM(shape[1:], jnp.float32),
            pltpu.VMEM(shape, jnp.bfloat16),
            pltpu.SemaphoreType.DMA,
            pltpu.SemaphoreType.DMA((6 * n,)),
            pltpu.SemaphoreType.DMA((2, n)),
        ],
        compiler_params=pltpu.CompilerParams(
            collective_id=0, has_side_effects=True, vmem_limit_bytes=16 * 1024 * 1024
        ),
    )(count, x, dest, blocks)


def transform(coef, put):
    cos = [math.cos(2 * math.pi * k / 16) for k in range(16)]
    sin = [math.sin(2 * math.pi * k / 16) for k in range(16)]
    a = [coef(0)] + [coef(2 * q) for q in range(1, 8)]
    b = [None] + [coef(2 * q + 1) for q in range(1, 8)]
    a8 = coef(1)
    s08, d08 = a[0] + a8, a[0] - a8
    ee = [s08 + a[4], d08 - b[4], s08 - a[4], d08 + b[4]]
    sa, da, sb, db = a[2] + a[6], a[2] - a[6], b[2] + b[6], b[2] - b[6]
    r = cos[2]
    eo = [sa, r * (da - sb), -db, -(r * (da + sb))]
    even = [ee[k] + eo[k] for k in range(4)] + [ee[k] - eo[k] for k in range(4)]
    p1, m1, p3, m3 = a[1] + a[7], a[1] - a[7], a[3] + a[5], a[3] - a[5]
    bp1, bm1, bp3, bm3 = b[1] + b[7], b[1] - b[7], b[3] + b[5], b[3] - b[5]
    for k in range(8):
        u1, u3 = (p1, p3) if k % 2 == 0 else (m1, m3)
        v1, v3 = (bm1, bm3) if k % 2 == 0 else (bp1, bp3)
        k3 = 3 * k % 16
        if k == 0:
            odd = u1 + u3
        elif k == 4:
            odd = v3 - v1
        else:
            odd = cos[k] * u1 - sin[k] * v1 + cos[k3] * u3 - sin[k3] * v3
        put(k, even[k] + odd)
        put(k + 8, even[k] - odd)


def stack_kernel(n, slots, chunk, all_ref, basis_ref, out_ref, pick, coefs, basis, basis_sems):
    step = pl.program_id(0)
    rows = slots * CH * CH
    depth = n * all_ref.shape[2]

    def fetch(q):
        return pltpu.make_async_copy(basis_ref.at[q], basis.at[q], basis_sems.at[q])

    @pl.when(step == 0)
    def _():
        for q in range(PAIRS):
            fetch(q).start()
        me = lax.axis_index("chan").astype(jnp.float32)
        slot = lax.broadcasted_iota(jnp.int32, (slots, 2 * BINS), 0).astype(jnp.float32)
        found_a = jnp.zeros((slots, 2 * BINS), jnp.float32)
        found_b = jnp.zeros((slots, 2 * BINS), jnp.float32)
        for d in range(n):
            lists = all_ref[d, RADIX].astype(jnp.float32)
            here = jnp.logical_and(lists[0:1] == me, lists[1:2] == slot)
            found_a = jnp.where(here, lists[2:3], found_a)
            found_b = jnp.where(here, lists[3:4], found_b)

        def spread(found):
            total = jnp.sum(found, axis=1, keepdims=True) - 1.0
            wide = jnp.broadcast_to(total, (slots, depth))
            wide = jnp.broadcast_to(wide[:, None, :], (slots, CH * CH, depth))
            return wide.reshape(rows, depth).astype(jnp.int32)

        row = lax.broadcasted_iota(jnp.int32, (rows, depth), 0)
        column = lax.broadcasted_iota(jnp.int32, (rows, depth), 1)
        channel = (column >> 4) * 8 + (column & 7)
        segment = (column >> 3) & 1
        for side, found in enumerate((found_a, found_b)):
            member = (row >> 2) & 3 if side == 0 else row & 3
            same = channel == spread(found) * CH + member
            for s in range(2):
                hit = jnp.where(jnp.logical_and(same, segment == s), 1.0, 0.0)
                k = (side * 2 + s) * rows
                pick[k : k + rows, :] = hit.astype(jnp.bfloat16)

    @pl.when(step < PAIRS)
    def _():
        crosses = []
        for k in range(2):
            white = all_ref[:, step * 2 + k].reshape(depth, 2 * BINS)
            found = jnp.dot(pick[...], white, preferred_element_type=jnp.float32)
            re, im = 0.0, 0.0
            for s in range(2):
                left = found[s * rows : (s + 1) * rows]
                right = found[(2 + s) * rows : (3 + s) * rows]
                l0, l1 = left[:, :BINS], left[:, BINS:]
                r0, r1 = right[:, :BINS], right[:, BINS:]
                re = re + (l0 * r0 + l1 * r1)
                im = im + (l1 * r0 - l0 * r1)
            crosses += [(re * 0.5).astype(jnp.bfloat16), (im * 0.5).astype(jnp.bfloat16)]
        cross = jnp.concatenate(crosses, axis=1)
        fetch(step).wait()
        coefs[step] = jnp.dot(cross, basis[step], preferred_element_type=jnp.float32)

    @pl.when(step >= PAIRS)
    def _():
        base = (step - PAIRS) * chunk

        def body(i, carry):
            for h in range(SPAN // 128):
                def coef(k):
                    col = (k % 2) * SPAN + h * 128
                    at = pl.ds(pl.multiple_of(base + i * 8, 8), 8)
                    return coefs[k // 2, at, col : col + 128]

                def put(na, value):
                    col = na * SPAN + h * 128
                    out_ref[pl.ds(pl.multiple_of(i * 8, 8), 8), col : col + 128] = value

                transform(coef, put)
            return carry

        lax.fori_loop(0, chunk // 8, body, 0)


def stack(n, slots, pieces, basis):
    rows = slots * CH * CH
    half = pieces.shape[2]
    chunk = 64
    return pl.pallas_call(
        functools.partial(stack_kernel, n, slots, chunk),
        out_shape=jax.ShapeDtypeStruct((rows, LAGS), jnp.float32),
        grid=(PAIRS + rows // chunk,),
        in_specs=[
            pl.BlockSpec(memory_space=pltpu.VMEM),
            pl.BlockSpec(memory_space=pltpu.HBM),
        ],
        out_specs=pl.BlockSpec((chunk, LAGS), lambda i: (jnp.maximum(i - PAIRS, 0), 0)),
        scratch_shapes=[
            pltpu.VMEM((4 * rows, n * half), jnp.bfloat16),
            pltpu.VMEM((PAIRS, rows, 2 * SPAN), jnp.float32),
            pltpu.VMEM(basis.shape, jnp.bfloat16),
            pltpu.SemaphoreType.DMA((PAIRS,)),
        ],
        compiler_params=pltpu.CompilerParams(vmem_limit_bytes=40 * 1024 * 1024),
    )(pieces, basis)


def shards(basis, spectra, pair_blocks, pair_dest, pair_count):
    slots = pair_dest.shape[0]
    n = lax.axis_size("chan")
    x = spectra.transpose(2, 0, 1, 3).reshape(-1, FREQ)
    pieces = gather(n, pair_count, x, pair_dest.T, pair_blocks.T)
    out = stack(n, slots, pieces, jnp.asarray(basis))
    return out.reshape(slots, CH * CH, LAGS)


def solution(mesh):
    in_specs = (
        P(None, ("parts", "chan"), None, None),
        P(("parts", "chan"), None),
        P(("parts", "chan"), None),
        P(("parts", "chan")),
    )
    out_specs = P(("parts", "chan"), None, None)
    return jax.shard_map(
        functools.partial(shards, stage_basis()),
        mesh=mesh,
        in_specs=in_specs,
        out_specs=out_specs,
        check_vma=False,
    )
```

```python
import functools
import math

import jax
import jax.numpy as jnp
import ml_dtypes
import numpy as np
from jax import lax
from jax.experimental import pallas as pl
from jax.experimental.pallas import tpu as pltpu
from jax.sharding import PartitionSpec as P

LAGS = 4096
FREQ = 2048
CH = 4
RADIX = 16
BINS = FREQ // RADIX
SPAN = LAGS // RADIX
PAIRS = RADIX // 2
MESH = pl.DeviceIdType.MESH


def stage_basis():
    fb = np.arange(BINS)
    nb = np.arange(SPAN)

    def parts(fa):
        f = fa + RADIX * fb
        weight = np.where(f == 0, 1.0, 2.0)[:, None] / (2.0 * math.sqrt(FREQ))
        angle = (f[:, None] * nb[None, :] % LAGS) * (2.0 * math.pi / LAGS)
        c, s = weight * np.cos(angle), weight * np.sin(angle)
        return np.concatenate([c, -s]), np.concatenate([s, c])

    out = np.zeros((PAIRS, 4 * BINS, 2 * SPAN))
    for q in range(PAIRS):
        low = parts(q)
        high = parts(RADIX - q if q else PAIRS)
        if q:
            out[q] = np.block([[low[0], low[1]], [high[0], -high[1]]])
        else:
            zero = np.zeros_like(low[0])
            out[q] = np.block([[low[0], zero], [zero, high[0]]])
    return out.astype(ml_dtypes.bfloat16)


def tile_of(fa):
    if fa % PAIRS == 0:
        return fa // PAIRS
    return 2 * fa if fa < PAIRS else 2 * (RADIX - fa) + 1


def fill_pick(n, slots, all_ref, pick):
    rows = slots * CH * CH
    depth = n * all_ref.shape[2]
    me = lax.axis_index("chan").astype(jnp.float32)
    slot = lax.broadcasted_iota(jnp.int32, (slots, 2 * BINS), 0).astype(jnp.float32)
    found_a = jnp.zeros((slots, 2 * BINS), jnp.float32)
    found_b = jnp.zeros((slots, 2 * BINS), jnp.float32)
    for d in range(n):
        lists = all_ref[d, RADIX].astype(jnp.float32)
        here = jnp.logical_and(lists[0:1] == me, lists[1:2] == slot)
        found_a = jnp.where(here, lists[2:3], found_a)
        found_b = jnp.where(here, lists[3:4], found_b)

    def spread(found):
        total = jnp.sum(found, axis=1, keepdims=True) - 1.0
        wide = jnp.broadcast_to(total, (slots, depth))
        wide = jnp.broadcast_to(wide[:, None, :], (slots, CH * CH, depth))
        return wide.reshape(rows, depth).astype(jnp.int32)

    row = lax.broadcasted_iota(jnp.int32, (rows, depth), 0)
    column = lax.broadcasted_iota(jnp.int32, (rows, depth), 1)
    channel = (column >> 4) * 8 + (column & 7)
    segment = (column >> 3) & 1
    for side, found in enumerate((found_a, found_b)):
        member = (row >> 2) & 3 if side == 0 else row & 3
        same = channel == spread(found) * CH + member
        for s in range(2):
            hit = jnp.where(jnp.logical_and(same, segment == s), 1.0, 0.0)
            k = (side * 2 + s) * rows
            pick[k : k + rows, :] = hit.astype(jnp.bfloat16)


def cross_step(rows, q, all_ref, pick, basis, coef_ref):
    depth = all_ref.shape[0] * all_ref.shape[2]
    crosses = []
    for k in range(2):
        white = all_ref[:, q * 2 + k].reshape(depth, 2 * BINS)
        found = jnp.dot(pick[...], white, preferred_element_type=jnp.float32)
        re, im = 0.0, 0.0
        for s in range(2):
            left = found[s * rows : (s + 1) * rows]
            right = found[(2 + s) * rows : (3 + s) * rows]
            l0, l1 = left[:, :BINS], left[:, BINS:]
            r0, r1 = right[:, :BINS], right[:, BINS:]
            re = re + (l0 * r0 + l1 * r1)
            im = im + (l1 * r0 - l0 * r1)
        crosses += [(re * 0.5).astype(jnp.bfloat16), (im * 0.5).astype(jnp.bfloat16)]
    cross = jnp.concatenate(crosses, axis=1)
    coef_ref[q] = jnp.dot(cross, basis[q], preferred_element_type=jnp.float32)


def gather_kernel(
    n,
    count_ref,
    x_ref,
    dest_ref,
    blocks_ref,
    basis_ref,
    coef_ref,
    all_ref,
    lists,
    piece,
    pick,
    basis,
    own_sem,
    basis_sems,
    send_sems,
    recv_sems,
):
    me = lax.axis_index("chan")
    nz = n // 4
    z, y, c = me // 4, (me // 2) % 2, me % 2
    always, up, down = None, z < nz - 1, z > 0

    def index(zz, yy, cc):
        return (zz * 2 + yy) * 2 + cc

    def under(condition, body):
        if condition is None:
            body()
        else:
            pl.when(condition)(body)

    other_y, other_c = index(z, 1 - y, c), index(z, y, 1 - c)
    above, below = index(z + 1, y, c), index(z - 1, y, c)
    partners = [(always, other_y), (always, other_c), (up, above), (down, below)]
    barrier = pltpu.get_barrier_semaphore()
    for condition, dev in partners:
        under(
            condition,
            lambda dev=dev: pl.semaphore_signal(
                barrier, inc=1, device_id={"chan": dev}, device_id_type=MESH
            ),
        )

    fetches = [
        pltpu.make_async_copy(
            basis_ref.at[pl.ds(4 * k, 4)], basis.at[pl.ds(4 * k, 4)], basis_sems.at[k]
        )
        for k in range(2)
    ]
    for fetch in fetches:
        fetch.start()

    slots = dest_ref.shape[1]
    used = lax.broadcasted_iota(jnp.int32, (1, slots), 1) < count_ref[0]
    lists[...] = jnp.full(lists.shape, -1.0, jnp.float32)
    lists[0:1, 0:slots] = jnp.where(used, dest_ref[0:1, :], -1).astype(jnp.float32)
    lists[1:2, 0:slots] = dest_ref[1:2, :].astype(jnp.float32)
    lists[2:4, 0:slots] = (blocks_ref[...] + 1).astype(jnp.float32)
    piece[RADIX] = lists[...].astype(jnp.bfloat16)
    rows = x_ref.shape[0]
    half = rows // 2
    values = x_ref[...].astype(jnp.float32)
    power = jnp.sum(values * values, axis=1, keepdims=True)
    mean_power = (power[:half] + power[half:]) * (1.0 / (2 * FREQ))
    root = jnp.sqrt(mean_power + 1e-06)
    white = (values / jnp.concatenate([root, root], axis=0)).astype(jnp.bfloat16)
    groups = FREQ // 256
    stacked = jnp.concatenate([white[:, g * 256 : (g + 1) * 256] for g in range(groups)], axis=0)
    src = lax.broadcasted_iota(jnp.int32, (256, 256), 0)
    dst = lax.broadcasted_iota(jnp.int32, (256, 256), 1)
    perm = ((src & 15) * 16 + (src >> 4) == dst).astype(jnp.float32).astype(jnp.bfloat16)
    sorted_bins = jnp.dot(stacked, perm, preferred_element_type=jnp.float32)
    place = lax.broadcasted_iota(jnp.int32, (rows, 128), 1) >> 4
    for h in range(2):
        turned = []
        for g in range(groups):
            t = sorted_bins[g * rows : (g + 1) * rows, h * 128 : (h + 1) * 128]
            turned.append(pltpu.roll(t, g * 16, 1) if g else t)
        for fl in range(8):
            t = turned[0]
            for g in range(1, groups):
                t = jnp.where(place == (fl + g) % 8, turned[g], t)
            if fl:
                t = pltpu.roll(t, 128 - fl * 16, 1)
            t = t.astype(jnp.bfloat16)
            piece[tile_of(h * 8 + fl), :, 0:128] = t[:half]
            piece[tile_of(h * 8 + fl), :, 128:256] = t[half:]

    own = pltpu.make_async_copy(piece, all_ref.at[me], own_sem)
    own.start()
    pl.semaphore_wait(barrier, 2 + (z + nz - 1) // nz + (2 * nz - 2 - z) // nz)
    halves = [pl.ds(PAIRS, PAIRS + 1), pl.ds(0, PAIRS)]
    copies = []

    def both(first, second):
        if first is None or second is None:
            return second if first is None else first
        return jnp.logical_and(first, second)

    def send(condition, k, what, dev, src_ref=None):
        copy = pltpu.make_async_remote_copy(
            src_ref=(all_ref.at[what] if src_ref is None else src_ref).at[halves[k]],
            dst_ref=all_ref.at[what, halves[k]],
            send_sem=send_sems.at[len(copies)],
            recv_sem=recv_sems.at[k, what],
            device_id={"chan": dev},
            device_id_type=MESH,
        )
        copies.append((condition, copy))
        under(condition, copy.start)

    def arrived(condition, k, what):
        under(
            condition,
            pltpu.make_async_remote_copy(
                src_ref=all_ref.at[what, halves[k]],
                dst_ref=all_ref.at[what, halves[k]],
                send_sem=send_sems.at[0],
                recv_sem=recv_sems.at[k, what],
                device_id={"chan": other_c},
                device_id_type=MESH,
            ).wait_recv,
        )

    for k in range(2):
        send(always, k, me, other_y, piece)
        send(up, k, me, above, piece)
        send(down, k, me, below, piece)
        send(always, k, me, other_c, piece)

    def z_step(t, k):
        for onward, there, zz, dev in (
            (up, z >= t, z - t, above),
            (down, z < nz - t, z + t, below),
        ):
            what = index(zz, y, c)
            arrived(there, k, what)
            send(there, k, what, other_y)
            if t < nz - 1:
                send(both(there, onward), k, what, dev)
            send(there, k, what, other_c)

    def y_step(t, k):
        if t == 1:
            arrived(always, k, other_y)
            send(always, k, other_y, other_c)
        else:
            for there, zz in ((z >= t - 1, z - t + 1), (z < nz - t + 1, z + t - 1)):
                what = index(zz, 1 - y, c)
                arrived(there, k, what)
                send(there, k, what, other_c)

    def c_wait(k):
        for zz in range(nz):
            for yy in range(2):
                arrived(always, k, index(zz, yy, 1 - c))

    rows = slots * CH * CH

    def cross_steps(low, high):
        def body(q, carry):
            cross_step(rows, q, all_ref, pick, basis, coef_ref)
            return carry

        lax.fori_loop(low, high, body, 0)

    for t in range(1, nz):
        z_step(t, 0)
        y_step(t, 0)
        if t > 1:
            z_step(t - 1, 1)
            y_step(t - 1, 1)
    y_step(nz, 0)
    z_step(nz - 1, 1)
    own.wait()
    for fetch in fetches:
        fetch.wait()
    c_wait(0)
    fill_pick(n, slots, all_ref, pick)
    cross_steps(6, 8)
    y_step(nz - 1, 1)
    y_step(nz, 1)
    cross_steps(4, 6)
    c_wait(1)
    cross_steps(0, 4)
    for condition, copy in copies:
        under(condition, copy.wait_send)


def limit(rows):
    return 60 * 1024 * 1024 - rows * LAGS * 8


def gather(n, count, x, dest, blocks, basis):
    half = x.shape[0] // 2
    rows = dest.shape[1] * CH * CH
    shape = (RADIX + 1, half, 2 * BINS)
    vmem = pl.BlockSpec(memory_space=pltpu.VMEM)
    hbm = pl.BlockSpec(memory_space=pltpu.HBM)
    return pl.pallas_call(
        functools.partial(gather_kernel, n),
        out_shape=jax.ShapeDtypeStruct((PAIRS, rows, 2 * SPAN), jnp.float32),
        in_specs=[pl.BlockSpec(memory_space=pltpu.SMEM), vmem, vmem, vmem, hbm],
        out_specs=vmem,
        scratch_shapes=[
            pltpu.VMEM((n,) + shape, jnp.bfloat16),
            pltpu.VMEM(shape[1:], jnp.float32),
            pltpu.VMEM(shape, jnp.bfloat16),
            pltpu.VMEM((4 * rows, n * half), jnp.bfloat16),
            pltpu.VMEM(basis.shape, jnp.bfloat16),
            pltpu.SemaphoreType.DMA,
            pltpu.SemaphoreType.DMA((2,)),
            pltpu.SemaphoreType.DMA((6 * n,)),
            pltpu.SemaphoreType.DMA((2, n)),
        ],
        compiler_params=pltpu.CompilerParams(
            collective_id=0, has_side_effects=True, vmem_limit_bytes=limit(rows)
        ),
    )(count, x, dest, blocks, basis)


def transform(coef, put):
    cos = [math.cos(2 * math.pi * k / 16) for k in range(16)]
    sin = [math.sin(2 * math.pi * k / 16) for k in range(16)]
    a = [coef(0)] + [coef(2 * q) for q in range(1, 8)]
    b = [None] + [coef(2 * q + 1) for q in range(1, 8)]
    a8 = coef(1)
    s08, d08 = a[0] + a8, a[0] - a8
    ee = [s08 + a[4], d08 - b[4], s08 - a[4], d08 + b[4]]
    sa, da, sb, db = a[2] + a[6], a[2] - a[6], b[2] + b[6], b[2] - b[6]
    r = cos[2]
    eo = [sa, r * (da - sb), -db, -(r * (da + sb))]
    even = [ee[k] + eo[k] for k in range(4)] + [ee[k] - eo[k] for k in range(4)]
    p1, m1, p3, m3 = a[1] + a[7], a[1] - a[7], a[3] + a[5], a[3] - a[5]
    bp1, bm1, bp3, bm3 = b[1] + b[7], b[1] - b[7], b[3] + b[5], b[3] - b[5]
    for k in range(8):
        u1, u3 = (p1, p3) if k % 2 == 0 else (m1, m3)
        v1, v3 = (bm1, bm3) if k % 2 == 0 else (bp1, bp3)
        k3 = 3 * k % 16
        if k == 0:
            odd = u1 + u3
        elif k == 4:
            odd = v3 - v1
        else:
            odd = cos[k] * u1 - sin[k] * v1 + cos[k3] * u3 - sin[k3] * v3
        put(k, even[k] + odd)
        put(k + 8, even[k] - odd)


def stack_kernel(chunk, coefs, out_ref):
    base = pl.program_id(0) * chunk

    def body(i, carry):
        for h in range(SPAN // 128):
            def coef(k):
                col = (k % 2) * SPAN + h * 128
                at = pl.ds(pl.multiple_of(base + i * 8, 8), 8)
                return coefs[k // 2, at, col : col + 128]

            def put(na, value):
                col = na * SPAN + h * 128
                out_ref[pl.ds(pl.multiple_of(i * 8, 8), 8), col : col + 128] = value

            transform(coef, put)
        return carry

    lax.fori_loop(0, chunk // 8, body, 0)


def stack(coefs):
    rows = coefs.shape[1]
    chunk = 32
    return pl.pallas_call(
        functools.partial(stack_kernel, chunk),
        out_shape=jax.ShapeDtypeStruct((rows, LAGS), jnp.float32),
        grid=(rows // chunk,),
        in_specs=[pl.BlockSpec(memory_space=pltpu.VMEM)],
        out_specs=pl.BlockSpec((chunk, LAGS), lambda i: (i, 0)),
        compiler_params=pltpu.CompilerParams(vmem_limit_bytes=16 * 1024 * 1024),
    )(coefs)


def shards(basis, spectra, pair_blocks, pair_dest, pair_count):
    slots = pair_dest.shape[0]
    n = lax.axis_size("chan")
    x = spectra.transpose(2, 0, 1, 3).reshape(-1, FREQ)
    coefs = gather(n, pair_count, x, pair_dest.T, pair_blocks.T, jnp.asarray(basis))
    out = stack(coefs)
    return out.reshape(slots, CH * CH, LAGS)


def solution(mesh):
    in_specs = (
        P(None, ("parts", "chan"), None, None),
        P(("parts", "chan"), None),
        P(("parts", "chan"), None),
        P(("parts", "chan")),
    )
    out_specs = P(("parts", "chan"), None, None)
    return jax.shard_map(
        functools.partial(shards, stage_basis()),
        mesh=mesh,
        in_specs=in_specs,
        out_specs=out_specs,
        check_vma=False,
    )
```

```python
import functools
import math

import jax
import jax.numpy as jnp
import ml_dtypes
import numpy as np
from jax import lax
from jax.experimental import pallas as pl
from jax.experimental.pallas import tpu as pltpu
from jax.sharding import PartitionSpec as P

LAGS = 4096
FREQ = 2048
CH = 4
RADIX = 16
BINS = FREQ // RADIX
SPAN = LAGS // RADIX
PAIRS = RADIX // 2
MESH = pl.DeviceIdType.MESH


def stage_basis():
    fb = np.arange(BINS)
    nb = np.arange(SPAN)

    def parts(fa):
        f = fa + RADIX * fb
        weight = np.where(f == 0, 1.0, 2.0)[:, None] / (2.0 * math.sqrt(FREQ))
        angle = (f[:, None] * nb[None, :] % LAGS) * (2.0 * math.pi / LAGS)
        c, s = weight * np.cos(angle), weight * np.sin(angle)
        return np.concatenate([c, -s]), np.concatenate([s, c])

    out = np.zeros((PAIRS, 4 * BINS, 2 * SPAN))
    for q in range(PAIRS):
        low = parts(q)
        high = parts(RADIX - q if q else PAIRS)
        if q:
            out[q] = np.block([[low[0], low[1]], [high[0], -high[1]]])
        else:
            zero = np.zeros_like(low[0])
            out[q] = np.block([[low[0], zero], [zero, high[0]]])
    return out.astype(ml_dtypes.bfloat16)


def tile_of(fa):
    if fa % PAIRS == 0:
        return fa // PAIRS
    return 2 * fa if fa < PAIRS else 2 * (RADIX - fa) + 1


def fill_pick(n, slots, all_ref, pick):
    rows = slots * CH * CH
    depth = n * all_ref.shape[2]
    me = lax.axis_index("chan").astype(jnp.float32)
    slot = lax.broadcasted_iota(jnp.int32, (slots, 2 * BINS), 0).astype(jnp.float32)
    found_a = jnp.zeros((slots, 2 * BINS), jnp.float32)
    found_b = jnp.zeros((slots, 2 * BINS), jnp.float32)
    for d in range(n):
        lists = all_ref[d, RADIX].astype(jnp.float32)
        here = jnp.logical_and(lists[0:1] == me, lists[1:2] == slot)
        found_a = jnp.where(here, lists[2:3], found_a)
        found_b = jnp.where(here, lists[3:4], found_b)

    def spread(found):
        total = jnp.sum(found, axis=1, keepdims=True) - 1.0
        wide = jnp.broadcast_to(total, (slots, depth))
        wide = jnp.broadcast_to(wide[:, None, :], (slots, CH * CH, depth))
        return wide.reshape(rows, depth).astype(jnp.int32)

    row = lax.broadcasted_iota(jnp.int32, (rows, depth), 0)
    column = lax.broadcasted_iota(jnp.int32, (rows, depth), 1)
    channel = (column >> 4) * 8 + (column & 7)
    segment = (column >> 3) & 1
    for side, found in enumerate((found_a, found_b)):
        member = (row >> 2) & 3 if side == 0 else row & 3
        same = channel == spread(found) * CH + member
        for s in range(2):
            hit = jnp.where(jnp.logical_and(same, segment == s), 1.0, 0.0)
            k = (side * 2 + s) * rows
            pick[k : k + rows, :] = hit.astype(jnp.bfloat16)


def cross_step(rows, q, all_ref, pick, basis, coef_ref):
    depth = all_ref.shape[0] * all_ref.shape[2]
    crosses = []
    for k in range(2):
        white = all_ref[:, q * 2 + k].reshape(depth, 2 * BINS)
        found = jnp.dot(pick[...], white, preferred_element_type=jnp.float32)
        re, im = 0.0, 0.0
        for s in range(2):
            left = found[s * rows : (s + 1) * rows]
            right = found[(2 + s) * rows : (3 + s) * rows]
            l0, l1 = left[:, :BINS], left[:, BINS:]
            r0, r1 = right[:, :BINS], right[:, BINS:]
            re = re + (l0 * r0 + l1 * r1)
            im = im + (l1 * r0 - l0 * r1)
        crosses += [(re * 0.5).astype(jnp.bfloat16), (im * 0.5).astype(jnp.bfloat16)]
    cross = jnp.concatenate(crosses, axis=1)
    coef_ref[q] = jnp.dot(cross, basis[q], preferred_element_type=jnp.float32)


def gather_kernel(
    n,
    count_ref,
    x_ref,
    pairs_ref,
    basis_ref,
    coef_ref,
    all_ref,
    lists,
    piece,
    pick,
    basis,
    own_sem,
    basis_sems,
    send_sems,
    recv_sems,
):
    me = lax.axis_index("chan")
    nz = n // 4
    z, y, c = me // 4, (me // 2) % 2, me % 2
    always, up, down = None, z < nz - 1, z > 0

    def index(zz, yy, cc):
        return (zz * 2 + yy) * 2 + cc

    def under(condition, body):
        if condition is None:
            body()
        else:
            pl.when(condition)(body)

    other_y, other_c = index(z, 1 - y, c), index(z, y, 1 - c)
    above, below = index(z + 1, y, c), index(z - 1, y, c)
    partners = [(always, other_y), (always, other_c), (up, above), (down, below)]
    barrier = pltpu.get_barrier_semaphore()
    for condition, dev in partners:
        under(
            condition,
            lambda dev=dev: pl.semaphore_signal(
                barrier, inc=1, device_id={"chan": dev}, device_id_type=MESH
            ),
        )

    fetches = [
        pltpu.make_async_copy(
            basis_ref.at[pl.ds(4 * k, 4)], basis.at[pl.ds(4 * k, 4)], basis_sems.at[k]
        )
        for k in range(2)
    ]
    for fetch in fetches:
        fetch.start()

    slots = pairs_ref.shape[1]
    used = lax.broadcasted_iota(jnp.int32, (1, slots), 1) < count_ref[0]
    lists[...] = jnp.full(lists.shape, -1.0, jnp.float32)
    lists[0:1, 0:slots] = jnp.where(used, pairs_ref[0:1, :], -1).astype(jnp.float32)
    lists[1:2, 0:slots] = pairs_ref[1:2, :].astype(jnp.float32)
    lists[2:4, 0:slots] = (pairs_ref[2:4, :] + 1).astype(jnp.float32)
    piece[RADIX] = lists[...].astype(jnp.bfloat16)
    rows = x_ref.shape[0]
    half = rows // 2
    values = x_ref[...].astype(jnp.float32)
    power = jnp.sum(values * values, axis=1, keepdims=True)
    mean_power = (power[:half] + power[half:]) * (1.0 / (2 * FREQ))
    root = jnp.sqrt(mean_power + 1e-06)
    white = (values / jnp.concatenate([root, root], axis=0)).astype(jnp.bfloat16)
    groups = FREQ // 256
    stacked = jnp.concatenate([white[:, g * 256 : (g + 1) * 256] for g in range(groups)], axis=0)
    src = lax.broadcasted_iota(jnp.int32, (256, 256), 0)
    dst = lax.broadcasted_iota(jnp.int32, (256, 256), 1)
    perm = ((src & 15) * 16 + (src >> 4) == dst).astype(jnp.float32).astype(jnp.bfloat16)
    sorted_bins = jnp.dot(stacked, perm, preferred_element_type=jnp.float32)
    place = lax.broadcasted_iota(jnp.int32, (rows, 128), 1) >> 4
    for h in range(2):
        turned = []
        for g in range(groups):
            t = sorted_bins[g * rows : (g + 1) * rows, h * 128 : (h + 1) * 128]
            turned.append(pltpu.roll(t, g * 16, 1) if g else t)
        for fl in range(8):
            t = turned[0]
            for g in range(1, groups):
                t = jnp.where(place == (fl + g) % 8, turned[g], t)
            if fl:
                t = pltpu.roll(t, 128 - fl * 16, 1)
            t = t.astype(jnp.bfloat16)
            piece[tile_of(h * 8 + fl), :, 0:128] = t[:half]
            piece[tile_of(h * 8 + fl), :, 128:256] = t[half:]

    own = pltpu.make_async_copy(piece, all_ref.at[me], own_sem)
    own.start()
    pl.semaphore_wait(barrier, 2 + (z + nz - 1) // nz + (2 * nz - 2 - z) // nz)
    halves = [pl.ds(PAIRS, PAIRS + 1), pl.ds(0, PAIRS)]
    copies = []

    def both(first, second):
        if first is None or second is None:
            return second if first is None else first
        return jnp.logical_and(first, second)

    def send(condition, k, what, dev, src_ref=None):
        copy = pltpu.make_async_remote_copy(
            src_ref=(all_ref.at[what] if src_ref is None else src_ref).at[halves[k]],
            dst_ref=all_ref.at[what, halves[k]],
            send_sem=send_sems.at[len(copies)],
            recv_sem=recv_sems.at[k, what],
            device_id={"chan": dev},
            device_id_type=MESH,
        )
        copies.append((condition, copy))
        under(condition, copy.start)

    def arrived(condition, k, what):
        under(
            condition,
            pltpu.make_async_remote_copy(
                src_ref=all_ref.at[what, halves[k]],
                dst_ref=all_ref.at[what, halves[k]],
                send_sem=send_sems.at[0],
                recv_sem=recv_sems.at[k, what],
                device_id={"chan": other_c},
                device_id_type=MESH,
            ).wait_recv,
        )

    for k in range(2):
        send(always, k, me, other_y, piece)
        send(up, k, me, above, piece)
        send(down, k, me, below, piece)
        send(always, k, me, other_c, piece)

    def z_step(t, k):
        for onward, there, zz, dev in (
            (up, z >= t, z - t, above),
            (down, z < nz - t, z + t, below),
        ):
            what = index(zz, y, c)
            arrived(there, k, what)
            send(there, k, what, other_y)
            if t < nz - 1:
                send(both(there, onward), k, what, dev)
            send(there, k, what, other_c)

    def y_step(t, k):
        if t == 1:
            arrived(always, k, other_y)
            send(always, k, other_y, other_c)
        else:
            for there, zz in ((z >= t - 1, z - t + 1), (z < nz - t + 1, z + t - 1)):
                what = index(zz, 1 - y, c)
                arrived(there, k, what)
                send(there, k, what, other_c)

    def c_wait(k):
        for zz in range(nz):
            for yy in range(2):
                arrived(always, k, index(zz, yy, 1 - c))

    rows = slots * CH * CH

    def cross_steps(low, high):
        def body(q, carry):
            cross_step(rows, q, all_ref, pick, basis, coef_ref)
            return carry

        lax.fori_loop(low, high, body, 0)

    for t in range(1, nz):
        z_step(t, 0)
        y_step(t, 0)
        if t > 1:
            z_step(t - 1, 1)
            y_step(t - 1, 1)
    y_step(nz, 0)
    z_step(nz - 1, 1)
    y_step(nz - 1, 1)
    own.wait()
    for fetch in fetches:
        fetch.wait()
    c_wait(0)
    fill_pick(n, slots, all_ref, pick)
    y_step(nz, 1)
    cross_steps(4, 8)
    c_wait(1)
    cross_steps(0, 4)
    for condition, copy in copies:
        under(condition, copy.wait_send)


def limit(rows):
    return 56 * 1024 * 1024 - rows * LAGS * 8


def gather(n, count, x, pairs, basis):
    half = x.shape[0] // 2
    rows = pairs.shape[1] * CH * CH
    shape = (RADIX + 1, half, 2 * BINS)
    vmem = pl.BlockSpec(memory_space=pltpu.VMEM)
    hbm = pl.BlockSpec(memory_space=pltpu.HBM)
    return pl.pallas_call(
        functools.partial(gather_kernel, n),
        out_shape=jax.ShapeDtypeStruct((PAIRS, rows, 2 * SPAN), jnp.float32),
        in_specs=[pl.BlockSpec(memory_space=pltpu.SMEM), vmem, vmem, hbm],
        out_specs=vmem,
        scratch_shapes=[
            pltpu.VMEM((n,) + shape, jnp.bfloat16),
            pltpu.VMEM(shape[1:], jnp.float32),
            pltpu.VMEM(shape, jnp.bfloat16),
            pltpu.VMEM((4 * rows, n * half), jnp.bfloat16),
            pltpu.VMEM(basis.shape, jnp.bfloat16),
            pltpu.SemaphoreType.DMA,
            pltpu.SemaphoreType.DMA((2,)),
            pltpu.SemaphoreType.DMA((6 * n,)),
            pltpu.SemaphoreType.DMA((2, n)),
        ],
        compiler_params=pltpu.CompilerParams(
            collective_id=0, has_side_effects=True, vmem_limit_bytes=limit(rows)
        ),
    )(count, x, pairs, basis)


def transform(coef, put):
    cos = [math.cos(2 * math.pi * k / 16) for k in range(16)]
    sin = [math.sin(2 * math.pi * k / 16) for k in range(16)]
    a = [coef(0)] + [coef(2 * q) for q in range(1, 8)]
    b = [None] + [coef(2 * q + 1) for q in range(1, 8)]
    a8 = coef(1)
    s08, d08 = a[0] + a8, a[0] - a8
    ee = [s08 + a[4], d08 - b[4], s08 - a[4], d08 + b[4]]
    sa, da, sb, db = a[2] + a[6], a[2] - a[6], b[2] + b[6], b[2] - b[6]
    r = cos[2]
    eo = [sa, r * (da - sb), -db, -(r * (da + sb))]
    even = [ee[k] + eo[k] for k in range(4)] + [ee[k] - eo[k] for k in range(4)]
    p1, m1, p3, m3 = a[1] + a[7], a[1] - a[7], a[3] + a[5], a[3] - a[5]
    bp1, bm1, bp3, bm3 = b[1] + b[7], b[1] - b[7], b[3] + b[5], b[3] - b[5]
    for k in range(8):
        u1, u3 = (p1, p3) if k % 2 == 0 else (m1, m3)
        v1, v3 = (bm1, bm3) if k % 2 == 0 else (bp1, bp3)
        k3 = 3 * k % 16
        if k == 0:
            odd = u1 + u3
        elif k == 4:
            odd = v3 - v1
        else:
            odd = cos[k] * u1 - sin[k] * v1 + cos[k3] * u3 - sin[k3] * v3
        put(k, even[k] + odd)
        put(k + 8, even[k] - odd)


def stack_kernel(chunk, coefs, out_ref):
    base = pl.program_id(0) * chunk

    def body(i, carry):
        for h in range(SPAN // 128):
            def coef(k):
                col = (k % 2) * SPAN + h * 128
                at = pl.ds(pl.multiple_of(base + i * 8, 8), 8)
                return coefs[k // 2, at, col : col + 128]

            def put(na, value):
                col = na * SPAN + h * 128
                out_ref[pl.ds(pl.multiple_of(i * 8, 8), 8), col : col + 128] = value

            transform(coef, put)
        return carry

    lax.fori_loop(0, chunk // 8, body, 0)


def stack(coefs):
    rows = coefs.shape[1]
    chunk = 32
    return pl.pallas_call(
        functools.partial(stack_kernel, chunk),
        out_shape=jax.ShapeDtypeStruct((rows, LAGS), jnp.float32),
        grid=(rows // chunk,),
        in_specs=[pl.BlockSpec(memory_space=pltpu.VMEM)],
        out_specs=pl.BlockSpec((chunk, LAGS), lambda i: (i, 0)),
        compiler_params=pltpu.CompilerParams(vmem_limit_bytes=16 * 1024 * 1024),
    )(coefs)


def shards(basis, spectra, pair_blocks, pair_dest, pair_count):
    slots = pair_dest.shape[0]
    n = lax.axis_size("chan")
    x = spectra.transpose(2, 0, 1, 3).reshape(-1, FREQ)
    pairs = jnp.concatenate([pair_dest.T, pair_blocks.T])
    coefs = gather(n, pair_count, x, pairs, jnp.asarray(basis))
    out = stack(coefs)
    return out.reshape(slots, CH * CH, LAGS)


def solution(mesh):
    in_specs = (
        P(None, ("parts", "chan"), None, None),
        P(("parts", "chan"), None),
        P(("parts", "chan"), None),
        P(("parts", "chan")),
    )
    out_specs = P(("parts", "chan"), None, None)
    return jax.shard_map(
        functools.partial(shards, stage_basis()),
        mesh=mesh,
        in_specs=in_specs,
        out_specs=out_specs,
        check_vma=False,
    )
```

```python
import functools
import math

import jax
import jax.numpy as jnp
import ml_dtypes
import numpy as np
from jax import lax
from jax.experimental import pallas as pl
from jax.experimental.pallas import tpu as pltpu
from jax.sharding import PartitionSpec as P

LAGS = 4096
FREQ = 2048
CH = 4
RADIX = 16
BINS = FREQ // RADIX
SPAN = LAGS // RADIX
PAIRS = RADIX // 2
MESH = pl.DeviceIdType.MESH


def stage_basis():
    fb = np.arange(BINS)
    nb = np.arange(SPAN)

    def parts(fa):
        f = fa + RADIX * fb
        weight = np.where(f == 0, 1.0, 2.0)[:, None] / (2.0 * math.sqrt(FREQ))
        angle = (f[:, None] * nb[None, :] % LAGS) * (2.0 * math.pi / LAGS)
        c, s = weight * np.cos(angle), weight * np.sin(angle)
        return np.concatenate([c, -s]), np.concatenate([s, c])

    out = np.zeros((PAIRS, 4 * BINS, 2 * SPAN))
    for q in range(PAIRS):
        low = parts(q)
        high = parts(RADIX - q if q else PAIRS)
        if q:
            out[q] = np.block([[low[0], low[1]], [high[0], -high[1]]])
        else:
            zero = np.zeros_like(low[0])
            out[q] = np.block([[low[0], zero], [zero, high[0]]])
    return out.astype(ml_dtypes.bfloat16)


def tile_of(fa):
    if fa % PAIRS == 0:
        return fa // PAIRS
    return 2 * fa if fa < PAIRS else 2 * (RADIX - fa) + 1


def fill_pick(n, slots, all_ref, pick):
    rows = slots * CH * CH
    depth = n * all_ref.shape[2]
    me = lax.axis_index("chan").astype(jnp.float32)
    slot = lax.broadcasted_iota(jnp.int32, (slots, 2 * BINS), 0).astype(jnp.float32)
    found_a = jnp.zeros((slots, 2 * BINS), jnp.float32)
    found_b = jnp.zeros((slots, 2 * BINS), jnp.float32)
    for d in range(n):
        lists = all_ref[d, RADIX].astype(jnp.float32)
        here = jnp.logical_and(lists[0:1] == me, lists[1:2] == slot)
        found_a = jnp.where(here, lists[2:3], found_a)
        found_b = jnp.where(here, lists[3:4], found_b)

    def spread(found):
        total = jnp.sum(found, axis=1, keepdims=True) - 1.0
        wide = jnp.broadcast_to(total, (slots, depth))
        wide = jnp.broadcast_to(wide[:, None, :], (slots, CH * CH, depth))
        return wide.reshape(rows, depth).astype(jnp.int32)

    row = lax.broadcasted_iota(jnp.int32, (rows, depth), 0)
    column = lax.broadcasted_iota(jnp.int32, (rows, depth), 1)
    channel = (column >> 4) * 8 + (column & 7)
    segment = (column >> 3) & 1
    for side, found in enumerate((found_a, found_b)):
        member = (row >> 2) & 3 if side == 0 else row & 3
        same = channel == spread(found) * CH + member
        for s in range(2):
            hit = jnp.where(jnp.logical_and(same, segment == s), 1.0, 0.0)
            k = (side * 2 + s) * rows
            pick[k : k + rows, :] = hit.astype(jnp.bfloat16)


def cross_step(rows, q, all_ref, pick, basis, coef_ref):
    depth = all_ref.shape[0] * all_ref.shape[2]
    crosses = []
    for k in range(2):
        white = all_ref[:, q * 2 + k].reshape(depth, 2 * BINS)
        found = jnp.dot(pick[...], white, preferred_element_type=jnp.float32)
        re, im = 0.0, 0.0
        for s in range(2):
            left = found[s * rows : (s + 1) * rows]
            right = found[(2 + s) * rows : (3 + s) * rows]
            l0, l1 = left[:, :BINS], left[:, BINS:]
            r0, r1 = right[:, :BINS], right[:, BINS:]
            re = re + (l0 * r0 + l1 * r1)
            im = im + (l1 * r0 - l0 * r1)
        crosses += [(re * 0.5).astype(jnp.bfloat16), (im * 0.5).astype(jnp.bfloat16)]
    cross = jnp.concatenate(crosses, axis=1)
    coef_ref[q] = jnp.dot(cross, basis[q], preferred_element_type=jnp.float32)


def gather_kernel(
    n,
    count_ref,
    x_ref,
    pairs_ref,
    basis_ref,
    coef_ref,
    all_ref,
    lists,
    piece,
    pick,
    basis,
    own_sem,
    basis_sems,
    send_sems,
    recv_sems,
):
    me = lax.axis_index("chan")
    nz = n // 4
    z, y, c = me // 4, (me // 2) % 2, me % 2
    always, up, down = None, z < nz - 1, z > 0

    def index(zz, yy, cc):
        return (zz * 2 + yy) * 2 + cc

    def under(condition, body):
        if condition is None:
            body()
        else:
            pl.when(condition)(body)

    other_y, other_c = index(z, 1 - y, c), index(z, y, 1 - c)
    above, below = index(z + 1, y, c), index(z - 1, y, c)
    partners = [(always, other_y), (always, other_c), (up, above), (down, below)]
    barrier = pltpu.get_barrier_semaphore()
    for condition, dev in partners:
        under(
            condition,
            lambda dev=dev: pl.semaphore_signal(
                barrier, inc=1, device_id={"chan": dev}, device_id_type=MESH
            ),
        )

    fetches = [
        pltpu.make_async_copy(
            basis_ref.at[pl.ds(4 * k, 4)], basis.at[pl.ds(4 * k, 4)], basis_sems.at[k]
        )
        for k in range(2)
    ]
    for fetch in fetches:
        fetch.start()

    slots = pairs_ref.shape[1]
    used = lax.broadcasted_iota(jnp.int32, (1, slots), 1) < count_ref[0]
    lists[...] = jnp.full(lists.shape, -1.0, jnp.float32)
    lists[0:1, 0:slots] = jnp.where(used, pairs_ref[0:1, :], -1).astype(jnp.float32)
    lists[1:2, 0:slots] = pairs_ref[1:2, :].astype(jnp.float32)
    lists[2:4, 0:slots] = (pairs_ref[2:4, :] + 1).astype(jnp.float32)
    piece[RADIX] = lists[...].astype(jnp.bfloat16)
    rows = x_ref.shape[0]
    half = rows // 2
    values = x_ref[...].astype(jnp.float32)
    power = jnp.sum(values * values, axis=1, keepdims=True)
    mean_power = (power[:half] + power[half:]) * (1.0 / (2 * FREQ))
    root = jnp.sqrt(mean_power + 1e-06)
    white = (values / jnp.concatenate([root, root], axis=0)).astype(jnp.bfloat16)
    groups = FREQ // 256
    stacked = jnp.concatenate([white[:, g * 256 : (g + 1) * 256] for g in range(groups)], axis=0)
    src = lax.broadcasted_iota(jnp.int32, (256, 256), 0)
    dst = lax.broadcasted_iota(jnp.int32, (256, 256), 1)
    perm = ((src & 15) * 16 + (src >> 4) == dst).astype(jnp.float32).astype(jnp.bfloat16)
    sorted_bins = jnp.dot(stacked, perm, preferred_element_type=jnp.float32)
    place = lax.broadcasted_iota(jnp.int32, (rows, 128), 1) >> 4
    for h in range(2):
        turned = []
        for g in range(groups):
            t = sorted_bins[g * rows : (g + 1) * rows, h * 128 : (h + 1) * 128]
            turned.append(pltpu.roll(t, g * 16, 1) if g else t)
        for fl in range(8):
            t = turned[0]
            for g in range(1, groups):
                t = jnp.where(place == (fl + g) % 8, turned[g], t)
            if fl:
                t = pltpu.roll(t, 128 - fl * 16, 1)
            t = t.astype(jnp.bfloat16)
            piece[tile_of(h * 8 + fl), :, 0:128] = t[:half]
            piece[tile_of(h * 8 + fl), :, 128:256] = t[half:]

    own = pltpu.make_async_copy(piece, all_ref.at[me], own_sem)
    own.start()
    pl.semaphore_wait(barrier, 2 + (z + nz - 1) // nz + (2 * nz - 2 - z) // nz)
    halves = [pl.ds(PAIRS, PAIRS + 1), pl.ds(0, PAIRS)]
    copies = []

    def both(first, second):
        if first is None or second is None:
            return second if first is None else first
        return jnp.logical_and(first, second)

    def send(condition, k, what, dev, src_ref=None):
        copy = pltpu.make_async_remote_copy(
            src_ref=(all_ref.at[what] if src_ref is None else src_ref).at[halves[k]],
            dst_ref=all_ref.at[what, halves[k]],
            send_sem=send_sems.at[len(copies)],
            recv_sem=recv_sems.at[k, what],
            device_id={"chan": dev},
            device_id_type=MESH,
        )
        copies.append((condition, copy))
        under(condition, copy.start)

    def arrived(condition, k, what):
        under(
            condition,
            pltpu.make_async_remote_copy(
                src_ref=all_ref.at[what, halves[k]],
                dst_ref=all_ref.at[what, halves[k]],
                send_sem=send_sems.at[0],
                recv_sem=recv_sems.at[k, what],
                device_id={"chan": other_c},
                device_id_type=MESH,
            ).wait_recv,
        )

    for k in range(2):
        send(always, k, me, other_y, piece)
        send(up, k, me, above, piece)
        send(down, k, me, below, piece)
        send(always, k, me, other_c, piece)

    def z_step(t, k):
        for onward, there, zz, dev in (
            (up, z >= t, z - t, above),
            (down, z < nz - t, z + t, below),
        ):
            what = index(zz, y, c)
            arrived(there, k, what)
            send(there, k, what, other_y)
            if t < nz - 1:
                send(both(there, onward), k, what, dev)
            send(there, k, what, other_c)

    def y_step(t, k):
        if t == 1:
            arrived(always, k, other_y)
            send(always, k, other_y, other_c)
        else:
            for there, zz in ((z >= t - 1, z - t + 1), (z < nz - t + 1, z + t - 1)):
                what = index(zz, 1 - y, c)
                arrived(there, k, what)
                send(there, k, what, other_c)

    def c_wait(k):
        for zz in range(nz):
            for yy in range(2):
                arrived(always, k, index(zz, yy, 1 - c))

    rows = slots * CH * CH

    def cross_steps(low, high):
        def body(q, carry):
            for k in range(2):
                cross_step(rows, 2 * q + k, all_ref, pick, basis, coef_ref)
            return carry

        lax.fori_loop(low // 2, high // 2, body, 0)

    for t in range(1, nz):
        z_step(t, 0)
        y_step(t, 0)
        if t > 1:
            z_step(t - 1, 1)
            y_step(t - 1, 1)
    y_step(nz, 0)
    z_step(nz - 1, 1)
    y_step(nz - 1, 1)
    own.wait()
    for fetch in fetches:
        fetch.wait()
    c_wait(0)
    fill_pick(n, slots, all_ref, pick)
    y_step(nz, 1)
    cross_steps(4, 8)
    c_wait(1)
    cross_steps(0, 4)
    for condition, copy in copies:
        under(condition, copy.wait_send)


def limit(rows):
    return 56 * 1024 * 1024 - rows * LAGS * 8


def gather(n, count, x, pairs, basis):
    half = x.shape[0] // 2
    rows = pairs.shape[1] * CH * CH
    shape = (RADIX + 1, half, 2 * BINS)
    vmem = pl.BlockSpec(memory_space=pltpu.VMEM)
    hbm = pl.BlockSpec(memory_space=pltpu.HBM)
    return pl.pallas_call(
        functools.partial(gather_kernel, n),
        out_shape=jax.ShapeDtypeStruct((PAIRS, rows, 2 * SPAN), jnp.float32),
        in_specs=[pl.BlockSpec(memory_space=pltpu.SMEM), vmem, vmem, hbm],
        out_specs=vmem,
        scratch_shapes=[
            pltpu.VMEM((n,) + shape, jnp.bfloat16),
            pltpu.VMEM(shape[1:], jnp.float32),
            pltpu.VMEM(shape, jnp.bfloat16),
            pltpu.VMEM((4 * rows, n * half), jnp.bfloat16),
            pltpu.VMEM(basis.shape, jnp.bfloat16),
            pltpu.SemaphoreType.DMA,
            pltpu.SemaphoreType.DMA((2,)),
            pltpu.SemaphoreType.DMA((6 * n,)),
            pltpu.SemaphoreType.DMA((2, n)),
        ],
        compiler_params=pltpu.CompilerParams(
            collective_id=0, has_side_effects=True, vmem_limit_bytes=limit(rows)
        ),
    )(count, x, pairs, basis)


def transform(coef, put):
    cos = [math.cos(2 * math.pi * k / 16) for k in range(16)]
    sin = [math.sin(2 * math.pi * k / 16) for k in range(16)]
    a = [coef(0)] + [coef(2 * q) for q in range(1, 8)]
    b = [None] + [coef(2 * q + 1) for q in range(1, 8)]
    a8 = coef(1)
    s08, d08 = a[0] + a8, a[0] - a8
    ee = [s08 + a[4], d08 - b[4], s08 - a[4], d08 + b[4]]
    sa, da, sb, db = a[2] + a[6], a[2] - a[6], b[2] + b[6], b[2] - b[6]
    r = cos[2]
    eo = [sa, r * (da - sb), -db, -(r * (da + sb))]
    even = [ee[k] + eo[k] for k in range(4)] + [ee[k] - eo[k] for k in range(4)]
    p1, m1, p3, m3 = a[1] + a[7], a[1] - a[7], a[3] + a[5], a[3] - a[5]
    bp1, bm1, bp3, bm3 = b[1] + b[7], b[1] - b[7], b[3] + b[5], b[3] - b[5]
    for k in range(8):
        u1, u3 = (p1, p3) if k % 2 == 0 else (m1, m3)
        v1, v3 = (bm1, bm3) if k % 2 == 0 else (bp1, bp3)
        k3 = 3 * k % 16
        if k == 0:
            odd = u1 + u3
        elif k == 4:
            odd = v3 - v1
        else:
            odd = cos[k] * u1 - sin[k] * v1 + cos[k3] * u3 - sin[k3] * v3
        put(k, even[k] + odd)
        put(k + 8, even[k] - odd)


def stack_kernel(chunk, coefs, out_ref):
    base = pl.program_id(0) * chunk

    def body(i, carry):
        for h in range(SPAN // 128):
            def coef(k):
                col = (k % 2) * SPAN + h * 128
                at = pl.ds(pl.multiple_of(base + i * 8, 8), 8)
                return coefs[k // 2, at, col : col + 128]

            def put(na, value):
                col = na * SPAN + h * 128
                out_ref[i * 8 : i * 8 + 8, col : col + 128] = value

            transform(coef, put)
        return carry

    for i in range(chunk // 8):
        body(i, 0)


def stack(coefs):
    rows = coefs.shape[1]
    chunk = 32
    return pl.pallas_call(
        functools.partial(stack_kernel, chunk),
        out_shape=jax.ShapeDtypeStruct((rows, LAGS), jnp.float32),
        grid=(rows // chunk,),
        in_specs=[pl.BlockSpec(memory_space=pltpu.VMEM)],
        out_specs=pl.BlockSpec((chunk, LAGS), lambda i: (i, 0)),
        compiler_params=pltpu.CompilerParams(vmem_limit_bytes=16 * 1024 * 1024),
    )(coefs)


def shards(basis, spectra, pair_blocks, pair_dest, pair_count):
    slots = pair_dest.shape[0]
    n = lax.axis_size("chan")
    x = spectra.transpose(2, 0, 1, 3).reshape(-1, FREQ)
    pairs = jnp.concatenate([pair_dest.T, pair_blocks.T])
    coefs = gather(n, pair_count, x, pairs, jnp.asarray(basis))
    out = stack(coefs)
    return out.reshape(slots, CH * CH, LAGS)


def solution(mesh):
    in_specs = (
        P(None, ("parts", "chan"), None, None),
        P(("parts", "chan"), None),
        P(("parts", "chan"), None),
        P(("parts", "chan")),
    )
    out_specs = P(("parts", "chan"), None, None)
    return jax.shard_map(
        functools.partial(shards, stage_basis()),
        mesh=mesh,
        in_specs=in_specs,
        out_specs=out_specs,
        check_vma=False,
    )
```
